128 devices in a mesh: sx: 8 (over y, z_hi), sy: 16 (over x, z_lo, core).
Axes of the slice: x: 4, y: 4, z: 4 (z_hi: 2, z_lo: 2; z = z_hi * 2 + z_lo), core: 2. Of those that a mesh axis runs over, the one named last changes fastest.
Arguments:
- panel: bfloat16 [8, 16, 64, 4096], P('sx', 'sy'), may hold values from -6 to 6
- band: bfloat16 [8, 16, 8, 3, 512, 512], P('sx', 'sy'), may hold values from -0.0024414062 to 0.0024414062
- faces: bfloat16 [8, 16, 4, 1024, 1024], P('sx', 'sy'), may hold values from -0.005859375 to 0.005859375
- face_rows: int32 [8, 16, 4, 1024], P('sx', 'sy'), may hold values from 0 to 4095
- owner: int32 [128], replicated, may hold values from 0 to 127, each once
Outputs:
- coarse_rows: float32 [128, 5, 4096], P(('sx', 'sy'))
The draws below stay inside these ranges and needn't reach their ends.
Inputs may be any that keep to these rules, and one draw needn't show every extreme that they name: owner names every index of 0 to 127 exactly once.
All inputs are finite; a program needn't handle non-finite values.
Results may differ from the reference program's by a relative error of at most 0.0029.
Values may be sent and summed in bfloat16 or wider, within the bound.
A program may use at most 128 MiB of HBM per device.

```python
import jax
import jax.numpy as jnp
from jax import lax

K = 64
TB = 512
NB = 8
F = 1024
R = 4096
NSUB = 128
N_SX = 8
N_SY = 16


def with_ends(entries, own_key, smallest, largest):
    place = [jax.random.randint(jax.random.fold_in(own_key, axis), (), 0, length) for axis, length in enumerate(entries.shape)]
    widest = entries.shape.index(max(entries.shape))
    neighbour = place[:widest] + [(place[widest] + 1) % entries.shape[widest]] + place[widest + 1:]
    return entries.at[tuple(place)].set(smallest).at[tuple(neighbour)].set(largest)


def levels(rng, shape, pieces, smallest, largest):
    def one(position, parts):
        draws = jax.random.uniform(jax.random.fold_in(jax.random.fold_in(rng, 6), position), (parts,), jnp.float32, smallest / len(pieces), largest / len(pieces))
        return jnp.repeat(jnp.exp(draws), shape[position] // parts).reshape((-1,) + (1,) * (len(shape) - position - 1))

    level = one(*pieces[0])
    for cut in pieces[1:]:
        level = level * one(*cut)
    return level


def noise(stream_key, extent, width, limit, split=(), held_as=jnp.bfloat16):
    result = width * jax.random.normal(stream_key, extent, jnp.float32)
    if split:
        result = result * levels(stream_key, extent, split, -0.22, 0.18)
    return jnp.clip(result, -limit, limit).astype(held_as)


def setup_inputs(seed: int = 0) -> dict:
    keys = jax.random.split(jax.random.key(seed), 6)
    return {
        "panel": noise(keys[0], (N_SX, N_SY, K, R), 1.0, 6.0, ((0, 8), (1, 16))),
        "band": noise(keys[1], (N_SX, N_SY, NB, 3, TB, TB), (3 * TB * R) ** -0.5, 0.0024414062, ((0, 8), (1, 16))),
        "faces": noise(keys[2], (N_SX, N_SY, 4, F, F), (F * F) ** -0.5, 0.005859375, ((0, 8), (1, 16))),
        "face_rows": with_ends(jax.random.randint(keys[3], (N_SX, N_SY, 4, F), 0, R), jax.random.fold_in(keys[3], 1), 0, R - 1).astype(jnp.int32),
        "owner": jax.random.permutation(keys[4], NSUB).astype(jnp.int32),
    }


def interior(vectors, band_tiles):
    count, tile = band_tiles.shape[0], band_tiles.shape[2]
    blocked = vectors.reshape(vectors.shape[0], count, tile)
    stacked = jnp.stack([jnp.roll(blocked, 1, axis=1), blocked, jnp.roll(blocked, -1, axis=1)], axis=1)
    applied = jnp.einsum("ktbj,btij->kbi", stacked.astype(jnp.float32), band_tiles.astype(jnp.float32))
    applied = applied.astype(jnp.bfloat16).reshape(vectors.shape)
    return lax.dot_general(vectors, applied, (((1,), (1,)), ((), ())), preferred_element_type=jnp.float32)


def face_blocks(vectors, face_tiles, face_index, remote):
    own_faces = jnp.take(vectors, face_index, axis=1)
    coupled = jnp.einsum("dkj,dij->dki", remote.astype(jnp.float32), face_tiles.astype(jnp.float32)).astype(jnp.bfloat16)
    return jnp.einsum("kdi,dli->dkl", own_faces.astype(jnp.float32), coupled.astype(jnp.float32))


def reference(panel, band, faces, face_rows, owner):
    padded_panel = jnp.pad(panel, ((1, 1), (1, 1), (0, 0), (0, 0)))
    padded_rows = jnp.pad(face_rows, ((1, 1), (1, 1), (0, 0), (0, 0)))

    def one_subdomain(index):
        xpos = index // N_SY
        ypos = index % N_SY
        vectors = panel[xpos, ypos]
        places = [(xpos, ypos + 1, 1), (xpos + 2, ypos + 1, 0), (xpos + 1, ypos, 3), (xpos + 1, ypos + 2, 2)]
        remote = jnp.stack([jnp.take(padded_panel[a, b], padded_rows[a, b, side], axis=1) for a, b, side in places])
        self_block = interior(vectors, band[xpos, ypos])
        others = face_blocks(vectors, faces[xpos, ypos], face_rows[xpos, ypos], remote)
        blocks = jnp.concatenate([self_block[None], others], axis=0)
        return blocks.reshape(5, K * K)

    blocks = lax.map(one_subdomain, jnp.arange(NSUB, dtype=jnp.int32))
    return jnp.zeros((NSUB, 5, K * K), jnp.float32).at[owner].set(blocks)
```

```python
import functools

import jax
import jax.numpy as jnp
from jax import lax
from jax.experimental import pallas as pl
from jax.experimental.pallas import tpu as pltpu
from jax.sharding import PartitionSpec as P

MESH = pl.DeviceIdType.MESH
F32, BF16 = jnp.float32, jnp.bfloat16
NX, NY = 8, 16
K, R, TB, NB, F = 64, 4096, 512, 8, 1024
TILES = 10


def dot_nn(a, b):
    return lax.dot_general(a, b, (((1,), (0,)), ((), ())), preferred_element_type=F32)


def dot_nt(a, b):
    return lax.dot_general(a, b, (((1,), (1,)), ((), ())), preferred_element_type=F32)


def split(value):
    high = value.astype(BF16)
    low = (value - high.astype(F32)).astype(BF16)
    return jnp.concatenate([high, low], axis=0)


def wait_bytes(ref, sem):
    pltpu.make_async_copy(ref, ref, sem).wait()


def kernel(
    panel, band, faces, rows, owner, out,
    pv, bv, fv, rv, ov, own, remote, pair, tmp, flat, recv1, pick, final,
    load_sem, send_sem, recv_sem, hop_send, hop_recv, ready,
):
    x, y = lax.axis_index("sx"), lax.axis_index("sy")
    me = x * NY + y

    loads = []

    def load(source, target):
        copy = pltpu.make_async_copy(source, target, load_sem.at[len(loads)])
        copy.start()
        loads.append(copy)
        return copy

    load_panel, load_rows, load_owner = load(panel, pv), load(rows, rv), load(owner, ov)
    load_band = [load(band.at[b], bv.at[b]) for b in range(NB)]
    load_faces = [load(faces.at[d], fv.at[d]) for d in range(4)]

    barrier = pltpu.get_barrier_semaphore()
    for step in range(1, NY):
        pl.semaphore_signal(barrier, inc=1, device_id=(x, lax.rem(y + step, NY)), device_id_type=MESH)
    for step in range(1, NX):
        pl.semaphore_signal(barrier, inc=1, device_id=(lax.rem(x + step, NX), y), device_id_type=MESH)

    has = [x > 0, x < NX - 1, y > 0, y < NY - 1]
    near = [(x - 1, y), (x + 1, y), (x, y - 1), (x, y + 1)]

    def exchange(d):
        return pltpu.make_async_remote_copy(
            src_ref=own.at[d], dst_ref=remote.at[d ^ 1], send_sem=send_sem.at[d], recv_sem=recv_sem.at[d ^ 1],
            device_id=near[d], device_id_type=MESH,
        )

    load_panel.wait()
    load_rows.wait()
    stacked = jnp.concatenate([pv[:, h * 256:(h + 1) * 256] for h in range(16)], axis=0)
    for d in range(4):
        for q in range(4):
            columns = slice(q * 256, (q + 1) * 256)
            index = rv[d:d + 1, columns]
            place, group = index & 255, index >> 8
            onehot = jnp.where(lax.broadcasted_iota(jnp.int32, (256, 256), 0) == place, 1.0, 0.0).astype(BF16)
            found = dot_nn(stacked, onehot)
            chosen = jnp.zeros((K, 256), F32)
            for h in range(16):
                chosen = jnp.where(group == h, found[h * K:(h + 1) * K], chosen)
            own[d, :, columns] = chosen.astype(BF16)
        if d == 0:
            pl.semaphore_wait(barrier, NX + NY - 2)
            for step in range(1, NX):
                pl.semaphore_signal(ready, inc=1, device_id=(lax.rem(x + step, NX), y), device_id_type=MESH)

        @pl.when(has[d])
        def _():
            exchange(d).start()

        @pl.when(jnp.logical_not(has[d]))
        def _():
            remote[d] = jnp.zeros((K, F), BF16)

    def put(b, block):
        tmp[:, :K] = block
        even = tmp[pl.ds(0, 32, 2), :]
        odd = tmp[pl.ds(1, 32, 2), :]
        flat[2 * b:2 * b + 2] = jnp.concatenate([even[:, :K], odd[:, :K]], axis=1).astype(BF16).reshape(2, 16, 128)

    total = jnp.zeros((2 * K, K), F32)
    waited = 0
    for c in [1, 2, 3, 4, 5, 6, 7, 0]:
        while waited < NB and waited <= c + 1:
            load_band[waited].wait()
            waited += 1
        product = None
        for t in range(3):
            b = (c + 1 - t) % NB
            term = dot_nn(pv[:, b * TB:(b + 1) * TB], bv[b, t])
            product = term if product is None else product + term
        total = total + dot_nt(split(product), pv[:, c * TB:(c + 1) * TB])
    put(0, total[:K] + total[K:])

    for d in range(4):
        load_faces[d].wait()
        for h in range(2):
            columns = slice(h * 512, (h + 1) * 512)
            pair[d, :, columns] = split(dot_nn(own[d], fv[d, :, columns]))

    load_owner.wait()
    targets = x * NY + lax.broadcasted_iota(jnp.int32, (NY, NX * NY), 0)
    sources = lax.broadcasted_iota(jnp.int32, (NY, NX * NY), 1)
    places = jnp.max(jnp.where(ov[...] == targets, sources, 0), axis=1, keepdims=True)
    places = [places[j, 0] for j in range(NY)]

    for d in (2, 3, 0, 1):
        @pl.when(has[d])
        def _():
            wait_bytes(remote.at[d], recv_sem.at[d])
        block = dot_nt(pair[d], remote[d])
        put(1 + d, block[:K] + block[K:])

    pl.semaphore_wait(ready, NX - 1)

    def first_hop(tile, step):
        return pltpu.make_async_remote_copy(
            src_ref=flat.at[tile], dst_ref=recv1.at[me], send_sem=hop_send.at[0], recv_sem=hop_recv.at[0],
            device_id=(lax.rem(x + step, NX), tile), device_id_type=MESH,
        )

    def send_tile(tile, _):
        for step in (4, 5, 3, 6, 2, 7, 1):
            first_hop(tile, step).start()

        @pl.when(tile != y)
        def _():
            first_hop(tile, 0).start()

        return 0

    lax.fori_loop(0, TILES, send_tile, 0)

    @pl.when(y < TILES)
    def _():
        recv1[me] = flat[y]
        wait_bytes(recv1.at[pl.ds(0, NX * NY - 1)], hop_recv.at[0])
        for j in range(NY):
            pick[j] = recv1[places[j]]
        for step in range(1, NY):
            to = lax.rem(y + step, NY)
            pltpu.make_async_remote_copy(
                src_ref=pick.at[to], dst_ref=final.at[y], send_sem=hop_send.at[1], recv_sem=hop_recv.at[1],
                device_id=(x, to), device_id_type=MESH,
            ).start()
        final[y] = pick[y]
        wait_bytes(final.at[pl.ds(0, TILES - 1)], hop_recv.at[1])

    @pl.when(y >= TILES)
    def _():
        wait_bytes(final, hop_recv.at[1])

    out[...] = final[...].astype(F32)

    for d in range(4):
        @pl.when(has[d])
        def _():
            wait_bytes(own.at[d], send_sem.at[d])

    @pl.when(y < TILES)
    def _():
        wait_bytes(recv1.at[pl.ds(0, NX * TILES - 1)], hop_send.at[0])
        wait_bytes(recv1.at[pl.ds(0, NY - 1)], hop_send.at[1])

    @pl.when(y >= TILES)
    def _():
        wait_bytes(recv1.at[pl.ds(0, NX * TILES)], hop_send.at[0])


def shards(panel, band, faces, face_rows, owner):
    blocks = pl.pallas_call(
        kernel,
        out_shape=jax.ShapeDtypeStruct((TILES, 16, 128), F32),
        in_specs=[pl.BlockSpec(memory_space=pl.ANY)] * 5,
        out_specs=pl.BlockSpec(memory_space=pltpu.VMEM),
        scratch_shapes=[
            pltpu.VMEM((K, R), BF16),
            pltpu.VMEM((NB, 3, TB, TB), BF16),
            pltpu.VMEM((4, F, F), BF16),
            pltpu.VMEM((4, F), jnp.int32),
            pltpu.VMEM((1, NX * NY), jnp.int32),
            pltpu.VMEM((4, K, F), BF16),
            pltpu.VMEM((4, K, F), BF16),
            pltpu.VMEM((4, 2 * K, F), BF16),
            pltpu.VMEM((K, 128), F32),
            pltpu.VMEM((TILES, 16, 128), BF16),
            pltpu.VMEM((NX * NY, 16, 128), BF16),
            pltpu.VMEM((NY, 16, 128), BF16),
            pltpu.VMEM((TILES, 16, 128), BF16),
            pltpu.SemaphoreType.DMA((3 + NB + 4,)),
            pltpu.SemaphoreType.DMA((4,)),
            pltpu.SemaphoreType.DMA((4,)),
            pltpu.SemaphoreType.DMA((2,)),
            pltpu.SemaphoreType.DMA((2,)),
            pltpu.SemaphoreType.REGULAR,
        ],
        compiler_params=pltpu.CompilerParams(collective_id=0, has_side_effects=True, vmem_limit_bytes=58 << 20),
        name="coarse_blocks",
    )(panel[0, 0], band[0, 0], faces[0, 0], face_rows[0, 0], owner.reshape(1, NX * NY))
    return blocks.reshape(1, 5, 4096)


def solution(mesh):
    in_specs = (
        P("sx", "sy", None, None),
        P("sx", "sy", None, None, None, None),
        P("sx", "sy", None, None, None),
        P("sx", "sy", None, None),
        P(),
    )
    out_specs = P(("sx", "sy"), None, None)
    return jax.shard_map(shards, mesh=mesh, in_specs=in_specs, out_specs=out_specs, check_vma=False)
```

```python
import functools

import jax
import jax.numpy as jnp
from jax import lax
from jax.experimental import pallas as pl
from jax.experimental.pallas import tpu as pltpu
from jax.sharding import PartitionSpec as P

MESH = pl.DeviceIdType.MESH
F32, BF16 = jnp.float32, jnp.bfloat16
NX, NY = 8, 16
K, R, TB, NB, F = 64, 4096, 512, 8, 1024
TILES = 10
PARTS = [(0, 2), (6, 4), (2, 4)]
STEPS = [
    ('gather', 0),
    ('gather', 1),
    ('greet',),
    ('exchange', 0),
    ('exchange', 1),
    ('gather', 2),
    ('gather', 3),
    ('exchange', 2),
    ('exchange', 3),
    ('band', 0, 8),
    ('put_band',),
    ('first', 0),
    ('face_loads', 0, 1, 2, 3),
    ('face', 0),
    ('face', 1),
    ('face', 2),
    ('face', 3),
    ('owners',),
    ('arrived', 2),
    ('arrived', 3),
    ('block', 2),
    ('block', 3),
    ('first', 1),
    ('arrived', 0),
    ('arrived', 1),
    ('block', 0),
    ('block', 1),
    ('first', 2),
    ('second', 0),
    ('second', 1),
    ('second', 2),
    ('finish', 0),
    ('finish', 1),
    ('finish', 2),
    ('drain',),
]
BAND_ORDER = [(1, 4), (2, 4), (3, 8), (4, 8), (5, 8), (6, 8), (7, 8), (0, 8)]
FAR_PLANE = [(2, 2), (2, 1), (2, 3), (1, 2), (3, 2), (2, 0), (0, 2), (1, 1), (1, 3), (3, 1), (3, 3), (1, 0), (3, 0), (0, 1), (0, 3)]
FAR_STACK = [4, 5, 2, 3, 6, 7, 1]
PLANE, STACK = 16, 8


def dot_nn(a, b):
    return lax.dot_general(a, b, (((1,), (0,)), ((), ())), preferred_element_type=F32)


def dot_nt(a, b):
    return lax.dot_general(a, b, (((1,), (1,)), ((), ())), preferred_element_type=F32)


def split(value):
    high = value.astype(BF16)
    low = (value - high.astype(F32)).astype(BF16)
    return jnp.concatenate([high, low], axis=0)


def wait_bytes(ref, sem):
    pltpu.make_async_copy(ref, ref, sem).wait()


def kernel(
    panel, band, faces, rows, owner, out,
    pv, bv, fv, rv, ov, own, remote, pair, tmp, flat, *refs,
):
    x, y = lax.axis_index("sx"), lax.axis_index("sy")
    me = x * NY + y
    planes, picks, stacks, sems = refs[:3], refs[3:6], refs[6:9], refs[9:]
    load_sem, send_sem, recv_sem, hop_send, hop_recv = sems
    loads = []

    def load(source, target):
        copy = pltpu.make_async_copy(source, target, load_sem.at[len(loads)])
        copy.start()
        loads.append(copy)
        return copy

    load_panel, load_rows = load(panel, pv), load(rows, rv)
    load_band = [load(band.at[b], bv.at[b]) for b in range(NB)]
    load_faces = [load(faces.at[d], fv.at[d]) for d in range(4)]
    load_owner = load(owner, ov)

    p, q = (y >> 2) * 4 + (x >> 1), (x & 1) * 4 + (y & 3)

    def in_plane(a, b):
        return lax.rem((x >> 1) + b, 4) * 2 + (x & 1), lax.rem((y >> 2) + a, 4) * 4 + (y & 3)

    def in_stack(bits):
        return x ^ (bits >> 2), y ^ (bits & 3)

    barrier = pltpu.get_barrier_semaphore()

    def hello(device):
        pl.semaphore_signal(barrier, inc=1, device_id=device, device_id_type=MESH)

    has = [x > 0, x < NX - 1, y > 0, y < NY - 1]
    near = [(x - 1, y), (x + 1, y), (x, y - 1), (x, y + 1)]
    beyond = [
        jnp.logical_and(has[0], (x & 1) == 0), jnp.logical_and(has[1], (x & 1) == 1),
        jnp.logical_and(has[2], (y & 3) == 0), jnp.logical_and(has[3], (y & 3) == 3),
    ]
    for d in range(4):
        pl.when(beyond[d])(lambda d=d: hello(near[d]))
    for bits in FAR_STACK:
        hello(in_stack(bits))
    for a, b in FAR_PLANE:
        hello(in_plane(a, b))

    def greet():
        pl.semaphore_wait(barrier, PLANE + STACK - 2 + sum(far.astype(jnp.int32) for far in beyond))

    def exchange(d):
        @pl.when(has[d])
        def _():
            pltpu.make_async_remote_copy(
                src_ref=own.at[d], dst_ref=remote.at[d ^ 1], send_sem=send_sem.at[d], recv_sem=recv_sem.at[d ^ 1],
                device_id=near[d], device_id_type=MESH,
            ).start()

    def arrived(d):
        @pl.when(has[d])
        def _():
            wait_bytes(remote.at[d], recv_sem.at[d])

    def gather(d):
        stacked = jnp.concatenate([pv[:, h * 256:(h + 1) * 256] for h in range(16)], axis=0)
        for q in range(4):
            columns = slice(q * 256, (q + 1) * 256)
            index = rv[d:d + 1, columns]
            place, group = index & 255, index >> 8
            onehot = jnp.where(lax.broadcasted_iota(jnp.int32, (256, 256), 0) == place, 1.0, 0.0).astype(BF16)
            found = dot_nn(stacked, onehot)
            chosen = jnp.zeros((K, 256), F32)
            for h in range(16):
                chosen = jnp.where(group == h, found[h * K:(h + 1) * K], chosen)
            own[d, :, columns] = chosen.astype(BF16)

    def put(b, block):
        tmp[:, :K] = block
        even = tmp[pl.ds(0, 32, 2), :]
        odd = tmp[pl.ds(1, 32, 2), :]
        flat[2 * b:2 * b + 2] = jnp.concatenate([even[:, :K], odd[:, :K]], axis=1).astype(BF16).reshape(2, 16, 128)

    state = {"total": jnp.zeros((2 * K, K), F32), "band": 0}

    def band_part(start, stop):
        for c, need in BAND_ORDER[start:stop]:
            while state["band"] < need:
                load_band[state["band"]].wait()
                state["band"] += 1
            product = None
            for t in range(3):
                b = (c + 1 - t) % NB
                term = dot_nn(pv[:, b * TB:(b + 1) * TB], bv[b, t])
                product = term if product is None else product + term
            state["total"] = state["total"] + dot_nt(split(product), pv[:, c * TB:(c + 1) * TB])

    def put_band():
        put(0, state["total"][:K] + state["total"][K:])

    def face_loads(*ds):
        for d in ds:
            load_faces[d].wait()

    def face_product(d):
        for h in range(2):
            columns = slice(h * 512, (h + 1) * 512)
            pair[d, :, columns] = split(dot_nn(own[d], fv[d, :, columns]))

    def face_block(d):
        block = dot_nt(pair[d], remote[d])
        put(1 + d, jnp.where(has[d], block[:K] + block[K:], 0.0))

    def owners():
        load_owner.wait()
        source = lax.broadcasted_iota(jnp.int32, (STACK, NX * NY), 1)
        source_p, source_q = ((source >> 2) & 3) * 4 + (source >> 5), ((source >> 4) & 1) * 4 + (source & 3)
        other = lax.broadcasted_iota(jnp.int32, (STACK, NX * NY), 0)
        target = ((x >> 1) * 2 + (other >> 2)) * NY + (y >> 2) * 4 + (other & 3)
        found = jnp.logical_and(ov[...] == target, source_q == q)
        places = jnp.max(jnp.where(found, source_p, 0), axis=1, keepdims=True)
        state["places"] = [places[j, 0] for j in range(STACK)]
        state["mine"] = jnp.max(jnp.where(ov[...] == me, source_q[:1], 0), axis=1, keepdims=True)[0, 0]

    def first_hop(part):
        tiles, plane = pl.ds(*PARTS[part]), planes[part]
        for a, b in FAR_PLANE:
            pltpu.make_async_remote_copy(
                src_ref=flat.at[tiles], dst_ref=plane.at[p],
                send_sem=hop_send.at[part], recv_sem=hop_recv.at[part],
                device_id=in_plane(a, b), device_id_type=MESH,
            ).start()
        plane[p] = flat[tiles]

    def second_hop(part):
        plane, pick, stack = planes[part], picks[part], stacks[part]
        wait_bytes(plane.at[pl.ds(0, PLANE - 1)], hop_recv.at[part])
        for j in range(STACK):
            pick[j] = plane[state["places"][j]]
        for bits in FAR_STACK:
            pltpu.make_async_remote_copy(
                src_ref=pick.at[q ^ bits], dst_ref=stack.at[q],
                send_sem=hop_send.at[3 + part], recv_sem=hop_recv.at[3 + part],
                device_id=in_stack(bits), device_id_type=MESH,
            ).start()
        stack[q] = pick[q]

    def finish(part):
        tiles, stack = pl.ds(*PARTS[part]), stacks[part]
        wait_bytes(stack.at[pl.ds(0, STACK - 1)], hop_recv.at[3 + part])
        out[tiles] = stack[state["mine"]].astype(F32)

    def drain():
        for d in range(4):
            @pl.when(has[d])
            def _():
                wait_bytes(own.at[d], send_sem.at[d])
        for part in range(len(PARTS)):
            wait_bytes(planes[part].at[pl.ds(0, PLANE - 1)], hop_send.at[part])
            wait_bytes(stacks[part].at[pl.ds(0, STACK - 1)], hop_send.at[3 + part])

    actions = dict(
        greet=greet, exchange=exchange, arrived=arrived, gather=gather, band=band_part, put_band=put_band,
        face_loads=face_loads, face=face_product, block=face_block, owners=owners, first=first_hop, second=second_hop,
        finish=finish, drain=drain,
    )
    load_panel.wait()
    load_rows.wait()
    for name, *numbers in STEPS:
        actions[name](*numbers)


def shards(panel, band, faces, face_rows, owner):
    blocks = pl.pallas_call(
        kernel,
        out_shape=jax.ShapeDtypeStruct((TILES, 16, 128), F32),
        in_specs=[pl.BlockSpec(memory_space=pl.ANY)] * 5,
        out_specs=pl.BlockSpec(memory_space=pltpu.VMEM),
        scratch_shapes=[
            pltpu.VMEM((K, R), BF16),
            pltpu.VMEM((NB, 3, TB, TB), BF16),
            pltpu.VMEM((4, F, F), BF16),
            pltpu.VMEM((4, F), jnp.int32),
            pltpu.VMEM((1, NX * NY), jnp.int32),
            pltpu.VMEM((4, K, F), BF16),
            pltpu.VMEM((4, K, F), BF16),
            pltpu.VMEM((4, 2 * K, F), BF16),
            pltpu.VMEM((K, 128), F32),
            pltpu.VMEM((TILES, 16, 128), BF16),
            *[pltpu.VMEM((PLANE, count, 16, 128), BF16) for _, count in PARTS],
            *[pltpu.VMEM((STACK, count, 16, 128), BF16) for _, count in PARTS * 2],
            pltpu.SemaphoreType.DMA((3 + NB + 4,)),
            pltpu.SemaphoreType.DMA((4,)),
            pltpu.SemaphoreType.DMA((4,)),
            pltpu.SemaphoreType.DMA((6,)),
            pltpu.SemaphoreType.DMA((6,)),
        ],
        compiler_params=pltpu.CompilerParams(collective_id=0, has_side_effects=True, vmem_limit_bytes=58 << 20),
        name="coarse_blocks",
    )(panel[0, 0], band[0, 0], faces[0, 0], face_rows[0, 0], owner.reshape(1, NX * NY))
    return blocks.reshape(1, 5, 4096)


def solution(mesh):
    in_specs = (
        P("sx", "sy", None, None),
        P("sx", "sy", None, None, None, None),
        P("sx", "sy", None, None, None),
        P("sx", "sy", None, None),
        P(),
    )
    out_specs = P(("sx", "sy"), None, None)
    return jax.shard_map(shards, mesh=mesh, in_specs=in_specs, out_specs=out_specs, check_vma=False)
```

```python
import functools

import jax
import jax.numpy as jnp
from jax import lax
from jax.experimental import pallas as pl
from jax.experimental.pallas import tpu as pltpu
from jax.sharding import PartitionSpec as P

MESH = pl.DeviceIdType.MESH
F32, BF16 = jnp.float32, jnp.bfloat16
OUT = BF16
NX, NY = 8, 16
K, R, TB, NB, F = 64, 4096, 512, 8, 1024
TILES = 10
ORDER = [0, 3, 4, 1, 2]
PARTS = [(0, 2, True), (2, 4, True), (6, 4, False)]
STEPS = [
    ('gather', 0),
    ('gather', 1),
    ('gather_if', 0, 2, 3),
    ('greet',),
    ('exchange', 0),
    ('exchange', 1),
    ('gather_if', 1, 2, 3),
    ('exchange', 2),
    ('exchange', 3),
    ('band', 0, 8),
    ('put_band',),
    ('first', 0),
    ('face_loads', 0, 1, 2, 3),
    ('face', 0),
    ('face', 1),
    ('face', 2),
    ('face', 3),
    ('owners',),
    ('arrived', 2),
    ('block', 2),
    ('arrived', 3),
    ('block', 3),
    ('first', 1),
    ('arrived', 0),
    ('block', 0),
    ('arrived', 1),
    ('block', 1),
    ('first', 2),
    ('second', 0),
    ('second', 2),
    ('second', 1),
    ('finish', 0),
    ('finish', 1),
    ('finish', 2),
    ('drain_faces', 0, 1, 2, 3),
    ('drain_parts', 0, 1, 2),
]
BAND_ORDER = [(1, 4), (2, 4), (3, 8), (4, 8), (5, 8), (6, 8), (7, 8), (0, 8)]
FAR_PLANE = [(2, 2), (2, 1), (2, 3), (1, 2), (3, 2), (2, 0), (0, 2), (1, 1), (1, 3), (3, 1), (3, 3), (1, 0), (3, 0), (0, 1), (0, 3)]
FAR_STACK = [4, 5, 2, 3, 6, 7, 1]
PLANE, STACK = 16, 8


def dot_nn(a, b):
    return lax.dot_general(a, b, (((1,), (0,)), ((), ())), preferred_element_type=F32)


def dot_nt(a, b):
    return lax.dot_general(a, b, (((1,), (1,)), ((), ())), preferred_element_type=F32)


def split(value):
    high = value.astype(BF16)
    low = (value - high.astype(F32)).astype(BF16)
    return jnp.concatenate([high, low], axis=0)


def wait_bytes(ref, sem):
    pltpu.make_async_copy(ref, ref, sem).wait()


def kernel(
    panel, band, faces, rows, owner, out,
    pv, bv, fv, rv, ov, own, remote, pair, tmp, flat, *refs,
):
    x, y = lax.axis_index("sx"), lax.axis_index("sy")
    me = x * NY + y
    n = len(PARTS)
    planes, picks, stacks, sems = refs[:n], refs[n:2 * n], refs[2 * n:3 * n], refs[3 * n:]
    load_sem, send_sem, recv_sem, hop_send, hop_recv = sems
    p, q = (y >> 2) * 4 + (x >> 1), (x & 1) * 4 + (y & 3)

    def in_plane(a, b):
        return lax.rem((x >> 1) + b, 4) * 2 + (x & 1), lax.rem((y >> 2) + a, 4) * 4 + (y & 3)

    def in_stack(bits):
        return x ^ (bits >> 2), y ^ (bits & 3)

    barrier = pltpu.get_barrier_semaphore()

    def hello(device):
        pl.semaphore_signal(barrier, inc=1, device_id=device, device_id_type=MESH)

    has = [x > 0, x < NX - 1, y > 0, y < NY - 1]
    near = [(x - 1, y), (x + 1, y), (x, y - 1), (x, y + 1)]
    beyond = [
        jnp.logical_and(has[0], (x & 1) == 0), jnp.logical_and(has[1], (x & 1) == 1),
        jnp.logical_and(has[2], (y & 3) == 0), jnp.logical_and(has[3], (y & 3) == 3),
    ]
    for d in range(4):
        pl.when(beyond[d])(lambda d=d: hello(near[d]))
    for bits in FAR_STACK:
        hello(in_stack(bits))

    loads = []

    def load(source, target):
        copy = pltpu.make_async_copy(source, target, load_sem.at[len(loads)])
        copy.start()
        loads.append(copy)
        return copy

    load_panel, load_rows = load(panel, pv), load(rows, rv)
    load_band = [load(band.at[b], bv.at[b]) for b in range(NB)]
    load_faces = [load(faces.at[d], fv.at[d]) for d in range(4)]
    load_owner = load(owner, ov)

    for a, b in FAR_PLANE:
        hello(in_plane(a, b))

    def greet():
        pl.semaphore_wait(barrier, PLANE + STACK - 2 + sum(far.astype(jnp.int32) for far in beyond))

    def exchange(d):
        @pl.when(has[d])
        def _():
            pltpu.make_async_remote_copy(
                src_ref=own.at[d], dst_ref=remote.at[d ^ 1], send_sem=send_sem.at[d], recv_sem=recv_sem.at[d ^ 1],
                device_id=near[d], device_id_type=MESH,
            ).start()

    def arrived(d):
        @pl.when(has[d])
        def _():
            wait_bytes(remote.at[d], recv_sem.at[d])

    def gather(d):
        stacked = jnp.concatenate([pv[:, h * 256:(h + 1) * 256] for h in range(16)], axis=0)
        for q in range(4):
            columns = slice(q * 256, (q + 1) * 256)
            index = rv[d:d + 1, columns]
            place, group = index & 255, index >> 8
            onehot = jnp.where(lax.broadcasted_iota(jnp.int32, (256, 256), 0) == place, 1.0, 0.0).astype(BF16)
            found = dot_nn(stacked, onehot)
            chosen = jnp.zeros((K, 256), F32)
            for h in range(16):
                chosen = jnp.where(group == h, found[h * K:(h + 1) * K], chosen)
            own[d, :, columns] = chosen.astype(BF16)

    late = (x & 1) == 1

    def gather_if(is_late, *ds):
        @pl.when(late if is_late else jnp.logical_not(late))
        def _():
            for d in ds:
                gather(d)

    def put(b, block):
        tmp[:, :K] = block
        even = tmp[pl.ds(0, 32, 2), :]
        odd = tmp[pl.ds(1, 32, 2), :]
        slot = 2 * ORDER.index(b)
        flat[slot:slot + 2] = jnp.concatenate([even[:, :K], odd[:, :K]], axis=1).astype(BF16).reshape(2, 16, 128)

    state = {"total": jnp.zeros((2 * K, K), F32), "band": 0}

    def band_part(start, stop):
        for c, need in BAND_ORDER[start:stop]:
            while state["band"] < need:
                load_band[state["band"]].wait()
                state["band"] += 1
            product = None
            for t in range(3):
                b = (c + 1 - t) % NB
                term = dot_nn(pv[:, b * TB:(b + 1) * TB], bv[b, t])
                product = term if product is None else product + term
            state["total"] = state["total"] + dot_nt(split(product), pv[:, c * TB:(c + 1) * TB])

    def put_band():
        put(0, state["total"][:K] + state["total"][K:])

    def face_loads(*ds):
        for d in ds:
            load_faces[d].wait()

    def face_product(d):
        for h in range(2):
            columns = slice(h * 512, (h + 1) * 512)
            pair[d, :, columns] = split(dot_nn(own[d], fv[d, :, columns]))

    def face_block(d):
        block = dot_nt(pair[d], remote[d])
        put(1 + d, jnp.where(has[d], block[:K] + block[K:], 0.0))

    def owners():
        load_owner.wait()
        source = lax.broadcasted_iota(jnp.int32, (PLANE, NX * NY), 1)
        source_p, source_q = ((source >> 2) & 3) * 4 + (source >> 5), ((source >> 4) & 1) * 4 + (source & 3)
        other = lax.broadcasted_iota(jnp.int32, (PLANE, NX * NY), 0)

        def latest(match, value):
            return jnp.max(jnp.where(match, value, 0), axis=1, keepdims=True)

        target = ((x >> 1) * 2 + ((other >> 2) & 1)) * NY + (y >> 2) * 4 + (other & 3)
        places = latest(jnp.logical_and(ov[...] == target, source_q == q), source_p)
        state["from_plane"] = [places[j, 0] for j in range(STACK)]
        target = ((other & 3) * 2 + (x & 1)) * NY + (other >> 2) * 4 + (y & 3)
        places = latest(jnp.logical_and(ov[...] == target, source_p == p), source_q)
        state["from_stack"] = [places[j, 0] for j in range(PLANE)]
        state["mine"] = [latest(ov[...] == me, value[:1])[0, 0] for value in (source_p, source_q)]

    def to_plane(source, target, sems):
        for a, b in FAR_PLANE:
            pltpu.make_async_remote_copy(
                src_ref=source(lax.rem((y >> 2) + a, 4) * 4 + lax.rem((x >> 1) + b, 4)), dst_ref=target.at[p],
                send_sem=hop_send.at[sems], recv_sem=hop_recv.at[sems], device_id=in_plane(a, b), device_id_type=MESH,
            ).start()

    def to_stack(source, target, sems):
        for bits in FAR_STACK:
            pltpu.make_async_remote_copy(
                src_ref=source(q ^ bits), dst_ref=target.at[q],
                send_sem=hop_send.at[sems], recv_sem=hop_recv.at[sems], device_id=in_stack(bits), device_id_type=MESH,
            ).start()

    def first_hop(part):
        first, count, plane_first = PARTS[part]
        tiles = pl.ds(first, count)
        if plane_first:
            to_plane(lambda other: flat.at[tiles], planes[part], part)
            planes[part][p] = flat[tiles]
        else:
            to_stack(lambda other: flat.at[tiles], stacks[part], part)
            stacks[part][q] = flat[tiles]

    def second_hop(part):
        plane, pick, stack = planes[part], picks[part], stacks[part]
        if PARTS[part][2]:
            wait_bytes(plane.at[pl.ds(0, PLANE - 1)], hop_recv.at[part])
            for j in range(STACK):
                pick[j] = plane[state["from_plane"][j]]
            to_stack(lambda other: pick.at[other], stack, n + part)
            stack[q] = pick[q]
        else:
            wait_bytes(stack.at[pl.ds(0, STACK - 1)], hop_recv.at[part])
            for j in range(PLANE):
                pick[j] = stack[state["from_stack"][j]]
            to_plane(lambda other: pick.at[other], plane, n + part)
            plane[p] = pick[p]

    def finish(part):
        first, count, plane_first = PARTS[part]
        if plane_first:
            wait_bytes(stacks[part].at[pl.ds(0, STACK - 1)], hop_recv.at[n + part])
            mine = stacks[part][state["mine"][1]].astype(OUT)
        else:
            wait_bytes(planes[part].at[pl.ds(0, PLANE - 1)], hop_recv.at[n + part])
            mine = planes[part][state["mine"][0]].astype(OUT)
        for i in range(0, count, 2):
            b = ORDER[(first + i) // 2]
            out[2 * b:2 * b + 2] = mine[i:i + 2]

    def drain_faces(*ds):
        for d in ds:
            @pl.when(has[d])
            def _():
                wait_bytes(own.at[d], send_sem.at[d])
    def drain_parts(*parts):
        for part in parts:
            plane_hop, stack_hop = (part, n + part) if PARTS[part][2] else (n + part, part)
            wait_bytes(planes[part].at[pl.ds(0, PLANE - 1)], hop_send.at[plane_hop])
            wait_bytes(stacks[part].at[pl.ds(0, STACK - 1)], hop_send.at[stack_hop])

    actions = dict(
        greet=greet, exchange=exchange, arrived=arrived, gather=gather, gather_if=gather_if, band=band_part, put_band=put_band,
        face_loads=face_loads, face=face_product, block=face_block, owners=owners, first=first_hop, second=second_hop,
        finish=finish, drain_faces=drain_faces, drain_parts=drain_parts,
    )
    load_panel.wait()
    load_rows.wait()
    for name, *numbers in STEPS:
        actions[name](*numbers)


def store(blocks, out):
    out[...] = blocks[...].astype(F32)


def shards(panel, band, faces, face_rows, owner):
    blocks = pl.pallas_call(
        kernel,
        out_shape=pltpu.VMEM((TILES, 16, 128), OUT),
        in_specs=[pl.BlockSpec(memory_space=pl.ANY)] * 5,
        out_specs=pl.BlockSpec(memory_space=pltpu.VMEM),
        scratch_shapes=[
            pltpu.VMEM((K, R), BF16),
            pltpu.VMEM((NB, 3, TB, TB), BF16),
            pltpu.VMEM((4, F, F), BF16),
            pltpu.VMEM((4, F), jnp.int32),
            pltpu.VMEM((1, NX * NY), jnp.int32),
            pltpu.VMEM((4, K, F), BF16),
            pltpu.VMEM((4, K, F), BF16),
            pltpu.VMEM((4, 2 * K, F), BF16),
            pltpu.VMEM((K, 128), F32),
            pltpu.VMEM((TILES, 16, 128), BF16),
            *[pltpu.VMEM((PLANE, count, 16, 128), BF16) for _, count, _ in PARTS * 2],
            *[pltpu.VMEM((STACK, count, 16, 128), BF16) for _, count, _ in PARTS],
            pltpu.SemaphoreType.DMA((3 + NB + 4,)),
            pltpu.SemaphoreType.DMA((4,)),
            pltpu.SemaphoreType.DMA((4,)),
            pltpu.SemaphoreType.DMA((2 * len(PARTS),)),
            pltpu.SemaphoreType.DMA((2 * len(PARTS),)),
        ],
        compiler_params=pltpu.CompilerParams(collective_id=0, has_side_effects=True, vmem_limit_bytes=58 << 20),
        name="coarse_blocks",
    )(panel[0, 0], band[0, 0], faces[0, 0], face_rows[0, 0], owner.reshape(1, NX * NY))
    rows = pl.pallas_call(
        store,
        out_shape=jax.ShapeDtypeStruct((TILES, 16, 128), F32),
        in_specs=[pl.BlockSpec(memory_space=pltpu.VMEM)],
        out_specs=pl.BlockSpec(memory_space=pltpu.VMEM),
        compiler_params=pltpu.CompilerParams(vmem_limit_bytes=1 << 20),
        name="store",
    )(blocks)
    return rows.reshape(1, 5, 4096)


def solution(mesh):
    in_specs = (
        P("sx", "sy", None, None),
        P("sx", "sy", None, None, None, None),
        P("sx", "sy", None, None, None),
        P("sx", "sy", None, None),
        P(),
    )
    out_specs = P(("sx", "sy"), None, None)
    return jax.shard_map(shards, mesh=mesh, in_specs=in_specs, out_specs=out_specs, check_vma=False)
```

```python
import functools

import jax
import jax.numpy as jnp
from jax import lax
from jax.experimental import pallas as pl
from jax.experimental.pallas import tpu as pltpu
from jax.sharding import PartitionSpec as P

MESH = pl.DeviceIdType.MESH
F32, BF16 = jnp.float32, jnp.bfloat16
OUT = BF16
NX, NY = 8, 16
K, R, TB, NB, F = 64, 4096, 512, 8, 1024
TILES = 10
ORDER = [0, 3, 4, 1, 2]
PARTS = [(0, 2, True), (2, 2, True), (4, 2, True), (6, 4, False)]
STEPS = [
    ('gather', 0),
    ('gather', 1),
    ('gather_if', 0, 2, 3),
    ('greet',),
    ('exchange', 0),
    ('exchange', 1),
    ('gather_if', 1, 2, 3),
    ('exchange', 2),
    ('exchange', 3),
    ('band', 0, 8),
    ('put_band',),
    ('first', 0),
    ('face_loads', 0, 1, 2, 3),
    ('face', 0),
    ('face', 1),
    ('face', 2),
    ('face', 3),
    ('near_block',),
    ('first', 1),
    ('owners',),
    ('arrived', 0),
    ('block', 0),
    ('arrived', 1),
    ('block', 1),
    ('first', 3),
    ('far_block',),
    ('first', 2),
    ('second', 0),
    ('second', 1),
    ('second', 3),
    ('second', 2),
    ('finish', 0),
    ('finish', 1),
    ('finish', 3),
    ('finish', 2),
    ('finish_y',),
    ('drain_faces', 0, 1, 2, 3),
    ('drain_parts', 0, 1, 2, 3),
]
BAND_ORDER = [(1, 4), (2, 4), (3, 8), (4, 8), (5, 8), (6, 8), (7, 8), (0, 8)]
FAR_PLANE = [(2, 2), (2, 1), (2, 3), (1, 2), (3, 2), (2, 0), (0, 2), (1, 1), (1, 3), (3, 1), (3, 3), (1, 0), (3, 0), (0, 1), (0, 3)]
FAR_STACK = [4, 5, 2, 3, 6, 7, 1]
PLANE, STACK = 16, 8


def dot_nn(a, b):
    return lax.dot_general(a, b, (((1,), (0,)), ((), ())), preferred_element_type=F32)


def dot_nt(a, b):
    return lax.dot_general(a, b, (((1,), (1,)), ((), ())), preferred_element_type=F32)


def split(value):
    high = value.astype(BF16)
    low = (value - high.astype(F32)).astype(BF16)
    return jnp.concatenate([high, low], axis=0)


def wait_bytes(ref, sem):
    pltpu.make_async_copy(ref, ref, sem).wait()


def kernel(
    panel, band, faces, rows, owner, out,
    pv, bv, fv, rv, ov, own, remote, pair, tmp, flat, *refs,
):
    x, y = lax.axis_index("sx"), lax.axis_index("sy")
    me = x * NY + y
    n = len(PARTS)
    planes, picks, stacks, sems = refs[:n], refs[n:2 * n], refs[2 * n:3 * n], refs[3 * n:]
    load_sem, send_sem, recv_sem, hop_send, hop_recv = sems
    p, q = (y >> 2) * 4 + (x >> 1), (x & 1) * 4 + (y & 3)

    def in_plane(a, b):
        return lax.rem((x >> 1) + b, 4) * 2 + (x & 1), lax.rem((y >> 2) + a, 4) * 4 + (y & 3)

    def in_stack(bits):
        return x ^ (bits >> 2), y ^ (bits & 3)

    barrier = pltpu.get_barrier_semaphore()

    def hello(device):
        pl.semaphore_signal(barrier, inc=1, device_id=device, device_id_type=MESH)

    has = [x > 0, x < NX - 1, y > 0, y < NY - 1]
    near = [(x - 1, y), (x + 1, y), (x, y - 1), (x, y + 1)]
    beyond = [
        jnp.logical_and(has[0], (x & 1) == 0), jnp.logical_and(has[1], (x & 1) == 1),
        jnp.logical_and(has[2], (y & 3) == 0), jnp.logical_and(has[3], (y & 3) == 3),
    ]
    for d in range(4):
        pl.when(beyond[d])(lambda d=d: hello(near[d]))
    for bits in FAR_STACK:
        hello(in_stack(bits))

    loads = []

    def load(source, target):
        copy = pltpu.make_async_copy(source, target, load_sem.at[len(loads)])
        copy.start()
        loads.append(copy)
        return copy

    load_panel, load_rows = load(panel, pv), load(rows, rv)
    load_band = [load(band.at[b], bv.at[b]) for b in range(NB)]
    load_faces = [load(faces.at[d], fv.at[d]) for d in range(4)]
    load_owner = load(owner, ov)

    for a, b in FAR_PLANE:
        hello(in_plane(a, b))

    def greet():
        pl.semaphore_wait(barrier, PLANE + STACK - 2 + sum(far.astype(jnp.int32) for far in beyond))

    def exchange(d):
        @pl.when(has[d])
        def _():
            pltpu.make_async_remote_copy(
                src_ref=own.at[d], dst_ref=remote.at[d ^ 1], send_sem=send_sem.at[d], recv_sem=recv_sem.at[d ^ 1],
                device_id=near[d], device_id_type=MESH,
            ).start()

    def arrived(d):
        @pl.when(has[d])
        def _():
            wait_bytes(remote.at[d], recv_sem.at[d])

    def gather(d):
        stacked = jnp.concatenate([pv[:, h * 256:(h + 1) * 256] for h in range(16)], axis=0)
        for q in range(4):
            columns = slice(q * 256, (q + 1) * 256)
            index = rv[d:d + 1, columns]
            place, group = index & 255, index >> 8
            onehot = jnp.where(lax.broadcasted_iota(jnp.int32, (256, 256), 0) == place, 1.0, 0.0).astype(BF16)
            found = dot_nn(stacked, onehot)
            chosen = jnp.zeros((K, 256), F32)
            for h in range(16):
                chosen = jnp.where(group == h, found[h * K:(h + 1) * K], chosen)
            own[d, :, columns] = chosen.astype(BF16)

    late = (x & 1) == 1

    def gather_if(is_late, *ds):
        @pl.when(late if is_late else jnp.logical_not(late))
        def _():
            for d in ds:
                gather(d)

    def put(b, block):
        tmp[:, :K] = block
        even = tmp[pl.ds(0, 32, 2), :]
        odd = tmp[pl.ds(1, 32, 2), :]
        slot = 2 * ORDER.index(b)
        flat[slot:slot + 2] = jnp.concatenate([even[:, :K], odd[:, :K]], axis=1).astype(BF16).reshape(2, 16, 128)

    state = {"total": jnp.zeros((2 * K, K), F32), "band": 0}

    def band_part(start, stop):
        for c, need in BAND_ORDER[start:stop]:
            while state["band"] < need:
                load_band[state["band"]].wait()
                state["band"] += 1
            product = None
            for t in range(3):
                b = (c + 1 - t) % NB
                term = dot_nn(pv[:, b * TB:(b + 1) * TB], bv[b, t])
                product = term if product is None else product + term
            state["total"] = state["total"] + dot_nt(split(product), pv[:, c * TB:(c + 1) * TB])

    def put_band():
        put(0, state["total"][:K] + state["total"][K:])

    def face_loads(*ds):
        for d in ds:
            load_faces[d].wait()

    def face_product(d):
        for h in range(2):
            columns = slice(h * 512, (h + 1) * 512)
            pair[d, :, columns] = split(dot_nn(own[d], fv[d, :, columns]))

    same_chip = 3 - (y & 1)
    other_chip = 5 - same_chip
    has_other = jnp.logical_and(y > 0, y < NY - 1)

    def near_block():
        wait_bytes(remote.at[same_chip], recv_sem.at[same_chip])
        block = dot_nt(pair[same_chip], remote[same_chip])
        put(3, block[:K] + block[K:])

    def far_block():
        @pl.when(has_other)
        def _():
            wait_bytes(remote.at[other_chip], recv_sem.at[other_chip])

        block = dot_nt(pair[other_chip], remote[other_chip])
        put(4, jnp.where(has_other, block[:K] + block[K:], 0.0))

    def face_block(d):
        block = dot_nt(pair[d], remote[d])
        put(1 + d, jnp.where(has[d], block[:K] + block[K:], 0.0))

    def owners():
        load_owner.wait()
        source = lax.broadcasted_iota(jnp.int32, (PLANE, NX * NY), 1)
        source_p, source_q = ((source >> 2) & 3) * 4 + (source >> 5), ((source >> 4) & 1) * 4 + (source & 3)
        other = lax.broadcasted_iota(jnp.int32, (PLANE, NX * NY), 0)

        def latest(match, value):
            return jnp.max(jnp.where(match, value, 0), axis=1, keepdims=True)

        target = ((x >> 1) * 2 + ((other >> 2) & 1)) * NY + (y >> 2) * 4 + (other & 3)
        places = latest(jnp.logical_and(ov[...] == target, source_q == q), source_p)
        state["from_plane"] = [places[j, 0] for j in range(STACK)]
        target = ((other & 3) * 2 + (x & 1)) * NY + (other >> 2) * 4 + (y & 3)
        places = latest(jnp.logical_and(ov[...] == target, source_p == p), source_q)
        state["from_stack"] = [places[j, 0] for j in range(PLANE)]
        state["mine"] = [latest(ov[...] == me, value[:1])[0, 0] for value in (source_p, source_q)]

    def to_plane(source, target, sems):
        for a, b in FAR_PLANE:
            pltpu.make_async_remote_copy(
                src_ref=source(lax.rem((y >> 2) + a, 4) * 4 + lax.rem((x >> 1) + b, 4)), dst_ref=target.at[p],
                send_sem=hop_send.at[sems], recv_sem=hop_recv.at[sems], device_id=in_plane(a, b), device_id_type=MESH,
            ).start()

    def to_stack(source, target, sems):
        for bits in FAR_STACK:
            pltpu.make_async_remote_copy(
                src_ref=source(q ^ bits), dst_ref=target.at[q],
                send_sem=hop_send.at[sems], recv_sem=hop_recv.at[sems], device_id=in_stack(bits), device_id_type=MESH,
            ).start()

    def first_hop(part):
        first, count, plane_first = PARTS[part]
        tiles = pl.ds(first, count)
        if plane_first:
            to_plane(lambda other: flat.at[tiles], planes[part], part)
            planes[part][p] = flat[tiles]
        else:
            to_stack(lambda other: flat.at[tiles], stacks[part], part)
            stacks[part][q] = flat[tiles]

    def second_hop(part):
        plane, pick, stack = planes[part], picks[part], stacks[part]
        if PARTS[part][2]:
            wait_bytes(plane.at[pl.ds(0, PLANE - 1)], hop_recv.at[part])
            for j in range(STACK):
                pick[j] = plane[state["from_plane"][j]]
            to_stack(lambda other: pick.at[other], stack, n + part)
            stack[q] = pick[q]
        else:
            wait_bytes(stack.at[pl.ds(0, STACK - 1)], hop_recv.at[part])
            for j in range(PLANE):
                pick[j] = stack[state["from_stack"][j]]
            to_plane(lambda other: pick.at[other], plane, n + part)
            plane[p] = pick[p]

    def finish(part):
        first, count, plane_first = PARTS[part]
        if plane_first:
            wait_bytes(stacks[part].at[pl.ds(0, STACK - 1)], hop_recv.at[n + part])
            mine = stacks[part][state["mine"][1]].astype(OUT)
        else:
            wait_bytes(planes[part].at[pl.ds(0, PLANE - 1)], hop_recv.at[n + part])
            mine = planes[part][state["mine"][0]].astype(OUT)
        for i in range(0, count, 2):
            b = ORDER[(first + i) // 2]
            if b in (3, 4):
                state[b] = mine[i:i + 2]
            else:
                out[2 * b:2 * b + 2] = mine[i:i + 2]

    def finish_y():
        lower_first = (jnp.zeros((2, 16, 128), jnp.int32) + state["mine"][1]) & 1 == 1
        near, far = state[3].astype(F32), state[4].astype(F32)
        out[6:8] = jnp.where(lower_first, near, far).astype(OUT)
        out[8:10] = jnp.where(lower_first, far, near).astype(OUT)

    def drain_faces(*ds):
        for d in ds:
            @pl.when(has[d])
            def _():
                wait_bytes(own.at[d], send_sem.at[d])
    def drain_parts(*parts):
        for part in parts:
            plane_hop, stack_hop = (part, n + part) if PARTS[part][2] else (n + part, part)
            wait_bytes(planes[part].at[pl.ds(0, PLANE - 1)], hop_send.at[plane_hop])
            wait_bytes(stacks[part].at[pl.ds(0, STACK - 1)], hop_send.at[stack_hop])

    actions = dict(
        greet=greet, exchange=exchange, arrived=arrived, gather=gather, gather_if=gather_if, band=band_part, put_band=put_band,
        face_loads=face_loads, face=face_product, block=face_block, owners=owners, first=first_hop, second=second_hop,
        finish=finish, drain_faces=drain_faces, near_block=near_block, far_block=far_block, finish_y=finish_y, drain_parts=drain_parts,
    )
    load_panel.wait()
    load_rows.wait()
    for name, *numbers in STEPS:
        actions[name](*numbers)


def store(blocks, out):
    out[...] = blocks[...].astype(F32)


def shards(panel, band, faces, face_rows, owner):
    blocks = pl.pallas_call(
        kernel,
        out_shape=pltpu.VMEM((TILES, 16, 128), OUT),
        in_specs=[pl.BlockSpec(memory_space=pl.ANY)] * 5,
        out_specs=pl.BlockSpec(memory_space=pltpu.VMEM),
        scratch_shapes=[
            pltpu.VMEM((K, R), BF16),
            pltpu.VMEM((NB, 3, TB, TB), BF16),
            pltpu.VMEM((4, F, F), BF16),
            pltpu.VMEM((4, F), jnp.int32),
            pltpu.VMEM((1, NX * NY), jnp.int32),
            pltpu.VMEM((4, K, F), BF16),
            pltpu.VMEM((4, K, F), BF16),
            pltpu.VMEM((4, 2 * K, F), BF16),
            pltpu.VMEM((K, 128), F32),
            pltpu.VMEM((TILES, 16, 128), BF16),
            *[pltpu.VMEM((PLANE, count, 16, 128), BF16) for _, count, _ in PARTS * 2],
            *[pltpu.VMEM((STACK, count, 16, 128), BF16) for _, count, _ in PARTS],
            pltpu.SemaphoreType.DMA((3 + NB + 4,)),
            pltpu.SemaphoreType.DMA((4,)),
            pltpu.SemaphoreType.DMA((4,)),
            pltpu.SemaphoreType.DMA((2 * len(PARTS),)),
            pltpu.SemaphoreType.DMA((2 * len(PARTS),)),
        ],
        compiler_params=pltpu.CompilerParams(collective_id=0, has_side_effects=True, vmem_limit_bytes=58 << 20),
        name="coarse_blocks",
    )(panel[0, 0], band[0, 0], faces[0, 0], face_rows[0, 0], owner.reshape(1, NX * NY))
    rows = pl.pallas_call(
        store,
        out_shape=jax.ShapeDtypeStruct((TILES, 16, 128), F32),
        in_specs=[pl.BlockSpec(memory_space=pltpu.VMEM)],
        out_specs=pl.BlockSpec(memory_space=pltpu.VMEM),
        compiler_params=pltpu.CompilerParams(vmem_limit_bytes=1 << 20),
        name="store",
    )(blocks)
    return rows.reshape(1, 5, 4096)


def solution(mesh):
    in_specs = (
        P("sx", "sy", None, None),
        P("sx", "sy", None, None, None, None),
        P("sx", "sy", None, None, None),
        P("sx", "sy", None, None),
        P(),
    )
    out_specs = P(("sx", "sy"), None, None)
    return jax.shard_map(shards, mesh=mesh, in_specs=in_specs, out_specs=out_specs, check_vma=False)
```

```python
import functools

import jax
import jax.numpy as jnp
from jax import lax
from jax.experimental import pallas as pl
from jax.experimental.pallas import tpu as pltpu
from jax.sharding import PartitionSpec as P

MESH = pl.DeviceIdType.MESH
F32, BF16 = jnp.float32, jnp.bfloat16
OUT = BF16
NX, NY = 8, 16
K, R, TB, NB, F = 64, 4096, 512, 8, 1024
TILES = 10
ORDER = [0, 3, 4, 1, 2]
PARTS = [(0, 2, True), (2, 2, True), (4, 2, True), (6, 4, False)]
STEPS = [
    ('gather', 0),
    ('gather', 1),
    ('gather_if', 0, 2, 3),
    ('greet',),
    ('exchange', 0),
    ('exchange', 1),
    ('gather_if', 1, 2, 3),
    ('exchange', 2),
    ('exchange', 3),
    ('band', 0, 8),
    ('put_band',),
    ('first', 0),
    ('face_loads', 0, 1, 2, 3),
    ('face_y', 1),
    ('near_block',),
    ('first', 1),
    ('face_y', 0),
    ('face', 0),
    ('face', 1),
    ('owners',),
    ('arrived', 0),
    ('arrived', 1),
    ('block', 0),
    ('block', 1),
    ('first', 3),
    ('far_block',),
    ('first', 2),
    ('second', 0),
    ('second', 1),
    ('second', 3),
    ('second', 2),
    ('finish', 0),
    ('finish', 1),
    ('finish', 3),
    ('finish', 2),
    ('finish_y',),
    ('drain_faces', 0, 1, 2, 3),
    ('drain_parts', 0, 1, 2, 3),
]
BAND_ORDER = [(1, 4), (2, 4), (3, 8), (4, 8), (5, 8), (6, 8), (7, 8), (0, 8)]
FAR_PLANE = [(2, 2), (2, 1), (2, 3), (1, 2), (3, 2), (2, 0), (0, 2), (1, 1), (1, 3), (3, 1), (3, 3), (1, 0), (3, 0), (0, 1), (0, 3)]
FAR_STACK = [4, 5, 2, 3, 6, 7, 1]
PLANE, STACK = 16, 8


def dot_nn(a, b):
    return lax.dot_general(a, b, (((1,), (0,)), ((), ())), preferred_element_type=F32)


def dot_nt(a, b):
    return lax.dot_general(a, b, (((1,), (1,)), ((), ())), preferred_element_type=F32)


def split(value):
    high = value.astype(BF16)
    low = (value - high.astype(F32)).astype(BF16)
    return jnp.concatenate([high, low], axis=0)


def wait_bytes(ref, sem):
    pltpu.make_async_copy(ref, ref, sem).wait()


def kernel(
    panel, band, faces, rows, owner, out,
    pv, bv, fv, rv, ov, own, remote, pair, tmp, flat, *refs,
):
    x, y = lax.axis_index("sx"), lax.axis_index("sy")
    me = x * NY + y
    n = len(PARTS)
    planes, picks, stacks, sems = refs[:n], refs[n:2 * n], refs[2 * n:3 * n], refs[3 * n:]
    load_sem, send_sem, recv_sem, hop_send, hop_recv = sems
    p, q = (y >> 2) * 4 + (x >> 1), (x & 1) * 4 + (y & 3)

    def in_plane(a, b):
        return lax.rem((x >> 1) + b, 4) * 2 + (x & 1), lax.rem((y >> 2) + a, 4) * 4 + (y & 3)

    def in_stack(bits):
        return x ^ (bits >> 2), y ^ (bits & 3)

    barrier = pltpu.get_barrier_semaphore()

    def hello(device):
        pl.semaphore_signal(barrier, inc=1, device_id=device, device_id_type=MESH)

    has = [x > 0, x < NX - 1, y > 0, y < NY - 1]
    near = [(x - 1, y), (x + 1, y), (x, y - 1), (x, y + 1)]
    beyond = [
        jnp.logical_and(has[0], (x & 1) == 0), jnp.logical_and(has[1], (x & 1) == 1),
        jnp.logical_and(has[2], (y & 3) == 0), jnp.logical_and(has[3], (y & 3) == 3),
    ]
    for d in range(4):
        pl.when(beyond[d])(lambda d=d: hello(near[d]))
    for bits in FAR_STACK:
        hello(in_stack(bits))

    loads = []

    def load(source, target):
        copy = pltpu.make_async_copy(source, target, load_sem.at[len(loads)])
        copy.start()
        loads.append(copy)
        return copy

    load_panel, load_rows = load(panel, pv), load(rows, rv)

    for a, b in FAR_PLANE:
        hello(in_plane(a, b))

    load_band = [load(band.at[b], bv.at[b]) for b in range(NB)]
    load_faces = [load(faces.at[d], fv.at[d]) for d in range(4)]
    load_owner = load(owner, ov)

    def greet():
        pl.semaphore_wait(barrier, PLANE + STACK - 2 + sum(far.astype(jnp.int32) for far in beyond))

    def exchange(d):
        @pl.when(has[d])
        def _():
            pltpu.make_async_remote_copy(
                src_ref=own.at[d], dst_ref=remote.at[d ^ 1], send_sem=send_sem.at[d], recv_sem=recv_sem.at[d ^ 1],
                device_id=near[d], device_id_type=MESH,
            ).start()

    def arrived(d):
        @pl.when(has[d])
        def _():
            wait_bytes(remote.at[d], recv_sem.at[d])

    def gather(d):
        stacked = jnp.concatenate([pv[:, h * 256:(h + 1) * 256] for h in range(16)], axis=0)
        for q in range(4):
            columns = slice(q * 256, (q + 1) * 256)
            index = rv[d:d + 1, columns]
            place, group = index & 255, index >> 8
            onehot = jnp.where(lax.broadcasted_iota(jnp.int32, (256, 256), 0) == place, 1.0, 0.0).astype(BF16)
            found = dot_nn(stacked, onehot)
            chosen = jnp.zeros((K, 256), F32)
            for h in range(16):
                chosen = jnp.where(group == h, found[h * K:(h + 1) * K], chosen)
            own[d, :, columns] = chosen.astype(BF16)

    late = (x & 1) == 1

    def gather_if(is_late, *ds):
        @pl.when(late if is_late else jnp.logical_not(late))
        def _():
            for d in ds:
                gather(d)

    def put(b, block):
        tmp[b, :, :K] = block
        even = tmp[b, pl.ds(0, 32, 2), :]
        odd = tmp[b, pl.ds(1, 32, 2), :]
        slot = 2 * ORDER.index(b)
        flat[slot:slot + 2] = jnp.concatenate([even[:, :K], odd[:, :K]], axis=1).astype(BF16).reshape(2, 16, 128)

    state = {"total": jnp.zeros((2 * K, K), F32), "band": 0}

    def band_part(start, stop):
        for c, need in BAND_ORDER[start:stop]:
            while state["band"] < need:
                load_band[state["band"]].wait()
                state["band"] += 1
            product = None
            for t in range(3):
                b = (c + 1 - t) % NB
                term = dot_nn(pv[:, b * TB:(b + 1) * TB], bv[b, t])
                product = term if product is None else product + term
            state["total"] = state["total"] + dot_nt(split(product), pv[:, c * TB:(c + 1) * TB])

    def put_band():
        put(0, state["total"][:K] + state["total"][K:])

    def face_loads(*ds):
        for d in ds:
            load_faces[d].wait()

    def face_product(d):
        for h in range(2):
            columns = slice(h * 512, (h + 1) * 512)
            pair[d, :, columns] = split(dot_nn(own[d], fv[d, :, columns]))

    same_chip = 3 - (y & 1)
    other_chip = 5 - same_chip
    has_other = jnp.logical_and(y > 0, y < NY - 1)

    def face_y(same):
        face_product(same_chip if same else other_chip)

    def near_block():
        wait_bytes(remote.at[same_chip], recv_sem.at[same_chip])
        block = dot_nt(pair[same_chip], remote[same_chip])
        put(3, block[:K] + block[K:])

    def far_block():
        @pl.when(has_other)
        def _():
            wait_bytes(remote.at[other_chip], recv_sem.at[other_chip])

        block = dot_nt(pair[other_chip], remote[other_chip])
        put(4, jnp.where(has_other, block[:K] + block[K:], 0.0))

    def face_block(d):
        block = dot_nt(pair[d], remote[d])
        put(1 + d, jnp.where(has[d], block[:K] + block[K:], 0.0))

    def owners():
        load_owner.wait()
        source = lax.broadcasted_iota(jnp.int32, (PLANE, NX * NY), 1)
        source_p, source_q = ((source >> 2) & 3) * 4 + (source >> 5), ((source >> 4) & 1) * 4 + (source & 3)
        other = lax.broadcasted_iota(jnp.int32, (PLANE, NX * NY), 0)

        def latest(match, value):
            return jnp.max(jnp.where(match, value, 0), axis=1, keepdims=True)

        target = ((x >> 1) * 2 + ((other >> 2) & 1)) * NY + (y >> 2) * 4 + (other & 3)
        places = latest(jnp.logical_and(ov[...] == target, source_q == q), source_p)
        state["from_plane"] = [places[j, 0] for j in range(STACK)]
        target = ((other & 3) * 2 + (x & 1)) * NY + (other >> 2) * 4 + (y & 3)
        places = latest(jnp.logical_and(ov[...] == target, source_p == p), source_q)
        state["from_stack"] = [places[j, 0] for j in range(PLANE)]
        state["mine"] = [latest(ov[...] == me, value[:1])[0, 0] for value in (source_p, source_q)]

    def to_plane(source, target, sems):
        for a, b in FAR_PLANE:
            pltpu.make_async_remote_copy(
                src_ref=source(lax.rem((y >> 2) + a, 4) * 4 + lax.rem((x >> 1) + b, 4)), dst_ref=target.at[p],
                send_sem=hop_send.at[sems], recv_sem=hop_recv.at[sems], device_id=in_plane(a, b), device_id_type=MESH,
            ).start()

    def to_stack(source, target, sems):
        for bits in FAR_STACK:
            pltpu.make_async_remote_copy(
                src_ref=source(q ^ bits), dst_ref=target.at[q],
                send_sem=hop_send.at[sems], recv_sem=hop_recv.at[sems], device_id=in_stack(bits), device_id_type=MESH,
            ).start()

    def first_hop(part):
        first, count, plane_first = PARTS[part]
        tiles = pl.ds(first, count)
        if plane_first:
            to_plane(lambda other: flat.at[tiles], planes[part], part)
            planes[part][p] = flat[tiles]
        else:
            to_stack(lambda other: flat.at[tiles], stacks[part], part)
            stacks[part][q] = flat[tiles]

    def second_hop(part):
        plane, pick, stack = planes[part], picks[part], stacks[part]
        if PARTS[part][2]:
            wait_bytes(plane.at[pl.ds(0, PLANE - 1)], hop_recv.at[part])
            for j in range(STACK):
                pick[j] = plane[state["from_plane"][j]]
            to_stack(lambda other: pick.at[other], stack, n + part)
            stack[q] = pick[q]
        else:
            wait_bytes(stack.at[pl.ds(0, STACK - 1)], hop_recv.at[part])
            for j in range(PLANE):
                pick[j] = stack[state["from_stack"][j]]
            to_plane(lambda other: pick.at[other], plane, n + part)
            plane[p] = pick[p]

    def finish(part):
        first, count, plane_first = PARTS[part]
        if plane_first:
            wait_bytes(stacks[part].at[pl.ds(0, STACK - 1)], hop_recv.at[n + part])
            mine = stacks[part][state["mine"][1]].astype(OUT)
        else:
            wait_bytes(planes[part].at[pl.ds(0, PLANE - 1)], hop_recv.at[n + part])
            mine = planes[part][state["mine"][0]].astype(OUT)
        for i in range(0, count, 2):
            b = ORDER[(first + i) // 2]
            if b in (3, 4):
                state[b] = mine[i:i + 2]
            else:
                out[2 * b:2 * b + 2] = mine[i:i + 2]

    def finish_y():
        lower_first = (jnp.zeros((2, 16, 128), jnp.int32) + state["mine"][1]) & 1 == 1
        near, far = state[3].astype(F32), state[4].astype(F32)
        out[6:8] = jnp.where(lower_first, near, far).astype(OUT)
        out[8:10] = jnp.where(lower_first, far, near).astype(OUT)

    def drain_faces(*ds):
        for d in ds:
            @pl.when(has[d])
            def _():
                wait_bytes(own.at[d], send_sem.at[d])
    def drain_parts(*parts):
        for part in parts:
            plane_hop, stack_hop = (part, n + part) if PARTS[part][2] else (n + part, part)
            wait_bytes(planes[part].at[pl.ds(0, PLANE - 1)], hop_send.at[plane_hop])
            wait_bytes(stacks[part].at[pl.ds(0, STACK - 1)], hop_send.at[stack_hop])

    actions = dict(
        greet=greet, exchange=exchange, arrived=arrived, gather=gather, gather_if=gather_if, band=band_part, put_band=put_band,
        face_loads=face_loads, face=face_product, block=face_block, owners=owners, first=first_hop, second=second_hop,
        finish=finish, drain_faces=drain_faces, near_block=near_block, face_y=face_y, far_block=far_block, finish_y=finish_y, drain_parts=drain_parts,
    )
    load_panel.wait()
    load_rows.wait()
    for name, *numbers in STEPS:
        actions[name](*numbers)


def store(blocks, out):
    out[...] = blocks[...].astype(F32)


def shards(panel, band, faces, face_rows, owner):
    blocks = pl.pallas_call(
        kernel,
        out_shape=pltpu.VMEM((TILES, 16, 128), OUT),
        in_specs=[pl.BlockSpec(memory_space=pl.ANY)] * 5,
        out_specs=pl.BlockSpec(memory_space=pltpu.VMEM),
        scratch_shapes=[
            pltpu.VMEM((K, R), BF16),
            pltpu.VMEM((NB, 3, TB, TB), BF16),
            pltpu.VMEM((4, F, F), BF16),
            pltpu.VMEM((4, F), jnp.int32),
            pltpu.VMEM((1, NX * NY), jnp.int32),
            pltpu.VMEM((4, K, F), BF16),
            pltpu.VMEM((4, K, F), BF16),
            pltpu.VMEM((4, 2 * K, F), BF16),
            pltpu.VMEM((5, K, 128), F32),
            pltpu.VMEM((TILES, 16, 128), BF16),
            *[pltpu.VMEM((PLANE, count, 16, 128), BF16) for _, count, _ in PARTS * 2],
            *[pltpu.VMEM((STACK, count, 16, 128), BF16) for _, count, _ in PARTS],
            pltpu.SemaphoreType.DMA((3 + NB + 4,)),
            pltpu.SemaphoreType.DMA((4,)),
            pltpu.SemaphoreType.DMA((4,)),
            pltpu.SemaphoreType.DMA((2 * len(PARTS),)),
            pltpu.SemaphoreType.DMA((2 * len(PARTS),)),
        ],
        compiler_params=pltpu.CompilerParams(collective_id=0, has_side_effects=True, vmem_limit_bytes=58 << 20),
        name="coarse_blocks",
    )(panel[0, 0], band[0, 0], faces[0, 0], face_rows[0, 0], owner.reshape(1, NX * NY))
    rows = pl.pallas_call(
        store,
        out_shape=jax.ShapeDtypeStruct((TILES, 16, 128), F32),
        in_specs=[pl.BlockSpec(memory_space=pltpu.VMEM)],
        out_specs=pl.BlockSpec(memory_space=pltpu.VMEM),
        compiler_params=pltpu.CompilerParams(vmem_limit_bytes=1 << 20),
        name="store",
    )(blocks)
    return rows.reshape(1, 5, 4096)


def solution(mesh):
    in_specs = (
        P("sx", "sy", None, None),
        P("sx", "sy", None, None, None, None),
        P("sx", "sy", None, None, None),
        P("sx", "sy", None, None),
        P(),
    )
    out_specs = P(("sx", "sy"), None, None)
    return jax.shard_map(shards, mesh=mesh, in_specs=in_specs, out_specs=out_specs, check_vma=False)
```

```python
import functools

import jax
import jax.numpy as jnp
from jax import lax
from jax.experimental import pallas as pl
from jax.experimental.pallas import tpu as pltpu
from jax.sharding import PartitionSpec as P

MESH = pl.DeviceIdType.MESH
F32, BF16 = jnp.float32, jnp.bfloat16
OUT = BF16
NX, NY = 8, 16
K, R, TB, NB, F = 64, 4096, 512, 8, 1024
TILES = 10
ORDER = [0, 3, 4, 1, 2]
PARTS = [(0, 2, True), (2, 2, True), (4, 2, True), (6, 4, False)]
STEPS = [
    ('gather', 0),
    ('gather', 1),
    ('gather_if', 0, 2, 3),
    ('greet',),
    ('exchange', 0),
    ('exchange', 1),
    ('gather_if', 1, 2, 3),
    ('exchange', 2),
    ('exchange', 3),
    ('band', 0, 8),
    ('put_band',),
    ('first', 0),
    ('face_loads', 0, 1, 2, 3),
    ('face_y', 1),
    ('near_block',),
    ('first', 1),
    ('face_y', 0),
    ('face', 0),
    ('face', 1),
    ('owners',),
    ('arrived', 0),
    ('arrived', 1),
    ('block', 0),
    ('block', 1),
    ('first', 3),
    ('far_block',),
    ('first', 2),
    ('second', 0),
    ('second', 1),
    ('second', 3),
    ('second', 2),
    ('finish', 0),
    ('finish', 1),
    ('finish', 3),
    ('finish', 2),
    ('finish_y',),
    ('drain_faces', 0, 1, 2, 3),
    ('drain_parts', 0, 1, 2, 3),
]
BAND_ORDER = [(1, 4), (2, 4), (3, 8), (4, 8), (5, 8), (6, 8), (7, 8), (0, 8)]
FAR_PLANE = [(2, 2), (2, 1), (2, 3), (1, 2), (3, 2), (2, 0), (0, 2), (1, 1), (1, 3), (3, 1), (3, 3), (1, 0), (3, 0), (0, 1), (0, 3)]
FAR_STACK = [4, 5, 2, 3, 6, 7, 1]
PLANE, STACK = 16, 8


def dot_nn(a, b):
    return lax.dot_general(a, b, (((1,), (0,)), ((), ())), preferred_element_type=F32)


def dot_nt(a, b):
    return lax.dot_general(a, b, (((1,), (1,)), ((), ())), preferred_element_type=F32)


def split(value):
    high = value.astype(BF16)
    low = (value - high.astype(F32)).astype(BF16)
    return jnp.concatenate([high, low], axis=0)


def wait_bytes(ref, sem):
    pltpu.make_async_copy(ref, ref, sem).wait()


def kernel(
    panel, band, faces, rows, owner, out,
    pv, bv, fv, rv, ov, own, remote, pair, tmp, flat, *refs,
):
    x, y = lax.axis_index("sx"), lax.axis_index("sy")
    me = x * NY + y
    n = len(PARTS)
    planes, picks, stacks, sems = refs[:n], refs[n:2 * n], refs[2 * n:3 * n], refs[3 * n:]
    load_sem, send_sem, recv_sem, hop_send, hop_recv = sems
    p, q = (y >> 2) * 4 + (x >> 1), (x & 1) * 4 + (y & 3)

    def in_plane(a, b):
        return (((x >> 1) + b) & 3) * 2 + (x & 1), (((y >> 2) + a) & 3) * 4 + (y & 3)

    def in_stack(bits):
        return x ^ (bits >> 2), y ^ (bits & 3)

    barrier = pltpu.get_barrier_semaphore()

    def hello(device):
        pl.semaphore_signal(barrier, inc=1, device_id=device, device_id_type=MESH)

    has = [x > 0, x < NX - 1, y > 0, y < NY - 1]
    near = [(x - 1, y), (x + 1, y), (x, y - 1), (x, y + 1)]
    beyond = [
        jnp.logical_and(has[0], (x & 1) == 0), jnp.logical_and(has[1], (x & 1) == 1),
        jnp.logical_and(has[2], (y & 3) == 0), jnp.logical_and(has[3], (y & 3) == 3),
    ]
    for d in range(4):
        pl.when(beyond[d])(lambda d=d: hello(near[d]))
    for bits in FAR_STACK:
        hello(in_stack(bits))

    loads = []

    def load(source, target):
        copy = pltpu.make_async_copy(source, target, load_sem.at[len(loads)])
        copy.start()
        loads.append(copy)
        return copy

    load_panel, load_rows = load(panel, pv), load(rows, rv)

    for a, b in FAR_PLANE:
        hello(in_plane(a, b))

    load_band = [load(band.at[b], bv.at[b]) for b in range(NB)]
    load_faces = [load(faces.at[d], fv.at[d]) for d in range(4)]
    load_owner = load(owner, ov)

    def greet():
        pl.semaphore_wait(barrier, PLANE + STACK - 2 + sum(far.astype(jnp.int32) for far in beyond))

    def exchange(d):
        @pl.when(has[d])
        def _():
            pltpu.make_async_remote_copy(
                src_ref=own.at[d], dst_ref=remote.at[d ^ 1], send_sem=send_sem.at[d], recv_sem=recv_sem.at[d ^ 1],
                device_id=near[d], device_id_type=MESH,
            ).start()

    def arrived(d):
        @pl.when(has[d])
        def _():
            wait_bytes(remote.at[d], recv_sem.at[d])

    def gather(d):
        stacked = jnp.concatenate([pv[:, h * 256:(h + 1) * 256] for h in range(16)], axis=0)
        for q in range(4):
            columns = slice(q * 256, (q + 1) * 256)
            index = rv[d:d + 1, columns]
            place, group = index & 255, index >> 8
            onehot = jnp.where(lax.broadcasted_iota(jnp.int32, (256, 256), 0) == place, 1.0, 0.0).astype(BF16)
            found = dot_nn(stacked, onehot)
            chosen = jnp.zeros((K, 256), F32)
            for h in range(16):
                chosen = jnp.where(group == h, found[h * K:(h + 1) * K], chosen)
            own[d, :, columns] = chosen.astype(BF16)

    late = (x & 1) == 1

    def gather_if(is_late, *ds):
        @pl.when(late if is_late else jnp.logical_not(late))
        def _():
            for d in ds:
                gather(d)

    def put(b, block):
        tmp[b, :, :K] = block
        even = tmp[b, pl.ds(0, 32, 2), :]
        odd = tmp[b, pl.ds(1, 32, 2), :]
        slot = 2 * ORDER.index(b)
        flat[slot:slot + 2] = jnp.concatenate([even[:, :K], odd[:, :K]], axis=1).astype(BF16).reshape(2, 16, 128)

    state = {"total": jnp.zeros((2 * K, K), F32), "band": 0}

    def band_part(start, stop):
        for c, need in BAND_ORDER[start:stop]:
            while state["band"] < need:
                load_band[state["band"]].wait()
                state["band"] += 1
            product = None
            for t in range(3):
                b = (c + 1 - t) % NB
                term = dot_nn(pv[:, b * TB:(b + 1) * TB], bv[b, t])
                product = term if product is None else product + term
            state["total"] = state["total"] + dot_nt(split(product), pv[:, c * TB:(c + 1) * TB])

    def put_band():
        put(0, state["total"][:K] + state["total"][K:])

    def face_loads(*ds):
        for d in ds:
            load_faces[d].wait()

    def face_product(d):
        for h in range(2):
            columns = slice(h * 512, (h + 1) * 512)
            pair[d, :, columns] = split(dot_nn(own[d], fv[d, :, columns]))

    same_chip = 3 - (y & 1)
    other_chip = 5 - same_chip
    has_other = jnp.logical_and(y > 0, y < NY - 1)

    def face_y(same):
        face_product(same_chip if same else other_chip)

    def near_block():
        wait_bytes(remote.at[same_chip], recv_sem.at[same_chip])
        block = dot_nt(pair[same_chip], remote[same_chip])
        put(3, block[:K] + block[K:])

    def far_block():
        @pl.when(has_other)
        def _():
            wait_bytes(remote.at[other_chip], recv_sem.at[other_chip])

        block = dot_nt(pair[other_chip], remote[other_chip])
        put(4, jnp.where(has_other, block[:K] + block[K:], 0.0))

    def face_block(d):
        block = dot_nt(pair[d], remote[d])
        put(1 + d, jnp.where(has[d], block[:K] + block[K:], 0.0))

    def owners():
        load_owner.wait()
        source = lax.broadcasted_iota(jnp.int32, (PLANE, NX * NY), 1)
        source_p, source_q = ((source >> 2) & 3) * 4 + (source >> 5), ((source >> 4) & 1) * 4 + (source & 3)
        other = lax.broadcasted_iota(jnp.int32, (PLANE, NX * NY), 0)

        def latest(match, value):
            return jnp.max(jnp.where(match, value, 0), axis=1, keepdims=True)

        target = ((x >> 1) * 2 + ((other >> 2) & 1)) * NY + (y >> 2) * 4 + (other & 3)
        places = latest(jnp.logical_and(ov[...] == target, source_q == q), source_p)
        state["from_plane"] = [places[j, 0] for j in range(STACK)]
        target = ((other & 3) * 2 + (x & 1)) * NY + (other >> 2) * 4 + (y & 3)
        places = latest(jnp.logical_and(ov[...] == target, source_p == p), source_q)
        state["from_stack"] = [places[j, 0] for j in range(PLANE)]
        state["mine"] = [latest(ov[...] == me, value[:1])[0, 0] for value in (source_p, source_q)]

    def to_plane(source, target, sems):
        for a, b in FAR_PLANE:
            pltpu.make_async_remote_copy(
                src_ref=source((((y >> 2) + a) & 3) * 4 + (((x >> 1) + b) & 3)), dst_ref=target.at[p],
                send_sem=hop_send.at[sems], recv_sem=hop_recv.at[sems], device_id=in_plane(a, b), device_id_type=MESH,
            ).start()

    def to_stack(source, target, sems):
        for bits in FAR_STACK:
            pltpu.make_async_remote_copy(
                src_ref=source(q ^ bits), dst_ref=target.at[q],
                send_sem=hop_send.at[sems], recv_sem=hop_recv.at[sems], device_id=in_stack(bits), device_id_type=MESH,
            ).start()

    def first_hop(part):
        first, count, plane_first = PARTS[part]
        tiles = pl.ds(first, count)
        if plane_first:
            to_plane(lambda other: flat.at[tiles], planes[part], part)
            planes[part][p] = flat[tiles]
        else:
            to_stack(lambda other: flat.at[tiles], stacks[part], part)
            stacks[part][q] = flat[tiles]

    def second_hop(part):
        plane, pick, stack = planes[part], picks[part], stacks[part]
        if PARTS[part][2]:
            wait_bytes(plane.at[pl.ds(0, PLANE - 1)], hop_recv.at[part])
            for j in range(STACK):
                pick[j] = plane[state["from_plane"][j]]
            to_stack(lambda other: pick.at[other], stack, n + part)
            stack[q] = pick[q]
        else:
            wait_bytes(stack.at[pl.ds(0, STACK - 1)], hop_recv.at[part])
            for j in range(PLANE):
                pick[j] = stack[state["from_stack"][j]]
            to_plane(lambda other: pick.at[other], plane, n + part)
            plane[p] = pick[p]

    def finish(part):
        first, count, plane_first = PARTS[part]
        if plane_first:
            wait_bytes(stacks[part].at[pl.ds(0, STACK - 1)], hop_recv.at[n + part])
            mine = stacks[part][state["mine"][1]].astype(OUT)
        else:
            wait_bytes(planes[part].at[pl.ds(0, PLANE - 1)], hop_recv.at[n + part])
            mine = planes[part][state["mine"][0]].astype(OUT)
        for i in range(0, count, 2):
            b = ORDER[(first + i) // 2]
            if b in (3, 4):
                state[b] = mine[i:i + 2]
            else:
                out[2 * b:2 * b + 2] = mine[i:i + 2]

    def finish_y():
        lower_first = (jnp.zeros((2, 16, 128), jnp.int32) + state["mine"][1]) & 1 == 1
        near, far = state[3].astype(F32), state[4].astype(F32)
        out[6:8] = jnp.where(lower_first, near, far).astype(OUT)
        out[8:10] = jnp.where(lower_first, far, near).astype(OUT)

    def drain_faces(*ds):
        for d in ds:
            @pl.when(has[d])
            def _():
                wait_bytes(own.at[d], send_sem.at[d])
    def drain_parts(*parts):
        for part in parts:
            plane_hop, stack_hop = (part, n + part) if PARTS[part][2] else (n + part, part)
            wait_bytes(planes[part].at[pl.ds(0, PLANE - 1)], hop_send.at[plane_hop])
            wait_bytes(stacks[part].at[pl.ds(0, STACK - 1)], hop_send.at[stack_hop])

    actions = dict(
        greet=greet, exchange=exchange, arrived=arrived, gather=gather, gather_if=gather_if, band=band_part, put_band=put_band,
        face_loads=face_loads, face=face_product, block=face_block, owners=owners, first=first_hop, second=second_hop,
        finish=finish, drain_faces=drain_faces, near_block=near_block, face_y=face_y, far_block=far_block, finish_y=finish_y, drain_parts=drain_parts,
    )
    load_panel.wait()
    load_rows.wait()
    for name, *numbers in STEPS:
        actions[name](*numbers)


def store(blocks, out):
    out[...] = blocks[...].astype(F32)


def shards(panel, band, faces, face_rows, owner):
    blocks = pl.pallas_call(
        kernel,
        out_shape=pltpu.VMEM((TILES, 16, 128), OUT),
        in_specs=[pl.BlockSpec(memory_space=pl.ANY)] * 5,
        out_specs=pl.BlockSpec(memory_space=pltpu.VMEM),
        scratch_shapes=[
            pltpu.VMEM((K, R), BF16),
            pltpu.VMEM((NB, 3, TB, TB), BF16),
            pltpu.VMEM((4, F, F), BF16),
            pltpu.VMEM((4, F), jnp.int32),
            pltpu.VMEM((1, NX * NY), jnp.int32),
            pltpu.VMEM((4, K, F), BF16),
            pltpu.VMEM((4, K, F), BF16),
            pltpu.VMEM((4, 2 * K, F), BF16),
            pltpu.VMEM((5, K, 128), F32),
            pltpu.VMEM((TILES, 16, 128), BF16),
            *[pltpu.VMEM((PLANE, count, 16, 128), BF16) for _, count, _ in PARTS * 2],
            *[pltpu.VMEM((STACK, count, 16, 128), BF16) for _, count, _ in PARTS],
            pltpu.SemaphoreType.DMA((3 + NB + 4,)),
            pltpu.SemaphoreType.DMA((4,)),
            pltpu.SemaphoreType.DMA((4,)),
            pltpu.SemaphoreType.DMA((2 * len(PARTS),)),
            pltpu.SemaphoreType.DMA((2 * len(PARTS),)),
        ],
        compiler_params=pltpu.CompilerParams(collective_id=0, has_side_effects=True, vmem_limit_bytes=58 << 20),
        name="coarse_blocks",
    )(panel[0, 0], band[0, 0], faces[0, 0], face_rows[0, 0], owner.reshape(1, NX * NY))
    rows = pl.pallas_call(
        store,
        out_shape=jax.ShapeDtypeStruct((TILES, 16, 128), F32),
        in_specs=[pl.BlockSpec(memory_space=pltpu.VMEM)],
        out_specs=pl.BlockSpec(memory_space=pltpu.VMEM),
        compiler_params=pltpu.CompilerParams(vmem_limit_bytes=1 << 20),
        name="store",
    )(blocks)
    return rows.reshape(1, 5, 4096)


def solution(mesh):
    in_specs = (
        P("sx", "sy", None, None),
        P("sx", "sy", None, None, None, None),
        P("sx", "sy", None, None, None),
        P("sx", "sy", None, None),
        P(),
    )
    out_specs = P(("sx", "sy"), None, None)
    return jax.shard_map(shards, mesh=mesh, in_specs=in_specs, out_specs=out_specs, check_vma=False)
```
